256 devices in a mesh: row: 16 (over x, z_hi), col: 16 (over z_lo, y, core).
Axes of the slice: x: 4, y: 4, z: 8 (z_hi: 4, z_lo: 2; z = z_hi * 2 + z_lo), core: 2. Of those that a mesh axis runs over, the one named last changes fastest.
Arguments:
- inputs: bfloat16 [2048, 8192], P('col', 'row'), may hold values from -6 to 6
- preact: bfloat16 [2048, 32768], P('row', 'col'), may hold values from -8 to 8
- out_grad: bfloat16 [2048, 32768], P('row', 'col'), may hold values from -0.796875 to 0.796875
- weight: bfloat16 [8192, 32768], P('row', 'col'), may hold values from -0.0625 to 0.0625
Outputs:
- input_grad: bfloat16 [2048, 8192], P('col', 'row')
- weight_grad: bfloat16 [8192, 32768], P('row', 'col')
The draws below stay inside these ranges and needn't reach their ends.
All inputs are finite; a program needn't handle non-finite values.
Results may differ from the reference program's by a relative error of at most 0.0049.
Values may be sent and summed in bfloat16 or wider, within the bound.
No kernel may reach another device: no remote copies, remote signals or barrier semaphores. Data moves between devices by JAX's collectives and lax.ppermute only.
A program may use at most 64 MiB of HBM per device.

```python
import math
import jax
import jax.numpy as jnp

D = 8192
FF = 32768
TOKENS = 2048


def levels(own_key, shape, pieces, low, top_value):
    loudness = 1.0
    for position, parts in pieces:
        draws = jax.random.uniform(jax.random.fold_in(jax.random.fold_in(own_key, 6), position), (parts,), jnp.float32, low / len(pieces), top_value / len(pieces))
        loudness = loudness * jnp.repeat(jnp.exp(draws), shape[position] // parts).reshape((-1,) + (1,) * (len(shape) - 1 - position))
    return loudness


def normal_values(rng, dims, spread, limit, shards=(), kind=jnp.bfloat16):
    gain = levels(rng, dims, shards, -0.22, 0.18) if shards else 1.0
    drawn = jax.random.normal(rng, dims, jnp.float32) * spread * gain
    return jnp.minimum(jnp.maximum(drawn, -limit), limit).astype(kind)


def setup_inputs(seed: int = 0) -> dict:
    seeds = jax.random.split(jax.random.key(seed), 5)
    return {
        "inputs": normal_values(seeds[0], (TOKENS, D), 1.0, 6.0, ((0, 16), (1, 16))),
        "preact": normal_values(seeds[1], (TOKENS, FF), 1.5, 8.0, ((0, 16), (1, 16))),
        "out_grad": normal_values(seeds[2], (TOKENS, FF), 0.1, 0.796875, ((0, 16), (1, 16))),
        "weight": normal_values(seeds[3], (D, FF), D ** -0.5, 0.0625, ((0, 16), (1, 16))),
    }


def gelu_slope(preact):
    h = preact.astype(jnp.float32)
    scale_c = math.sqrt(2.0 / math.pi)
    t = jnp.tanh(scale_c * (h + 0.044715 * h * h * h))
    return 0.5 * (1.0 + t) + 0.5 * h * (1.0 - t * t) * scale_c * (1.0 + 3.0 * 0.044715 * h * h)

def reference(inputs, preact, out_grad, weight):
    grad = (out_grad.astype(jnp.float32) * gelu_slope(preact)).astype(jnp.bfloat16)
    input_grad = jnp.dot(grad, weight.T, preferred_element_type=jnp.float32).astype(jnp.bfloat16)
    weight_grad = jnp.dot(inputs.T, grad, preferred_element_type=jnp.float32).astype(jnp.bfloat16)
    return (input_grad, weight_grad)
```

```python
import math

import jax
import jax.numpy as jnp
from jax import lax
from jax.experimental import pallas as pl
from jax.experimental.pallas import tpu as pltpu
from jax.sharding import PartitionSpec as P

ROWS = 128
NZ = 96
NX = ROWS - NZ
VMEM_LIMIT = 56 * 1024 * 1024

ORDER_Z = ((0, 0), (1, 0), (3, 0), (2, 0), (0, 1), (0, 3), (0, 2), (2, 2),
           (1, 1), (1, 3), (3, 1), (3, 3), (1, 2), (2, 1), (3, 2), (2, 3))
ORDER_X = tuple((dx, dz) for dz in (0, 1, 3, 2) for dx in (0, 1, 3, 2))


def gelu_slope(preact):
    h = preact.astype(jnp.float32)
    scale_c = math.sqrt(2.0 / math.pi)
    t = jnp.tanh(scale_c * (h + 0.044715 * h * h * h))
    return 0.5 * (1.0 + t) + 0.5 * h * (1.0 - t * t) * scale_c * (1.0 + 3.0 * 0.044715 * h * h)


def along_row(a, dx, dz):
    perm = [(x * 4 + z, (x + dx) % 4 * 4 + (z + dz) % 4) for x in range(4) for z in range(4)]
    return lax.ppermute(a, "row", perm)


def along_col(a, dl, dy, dc):
    perm = [
        (l * 8 + y * 2 + c, (l + dl) % 2 * 8 + (y + dy) % 4 * 2 + (c + dc) % 2)
        for l in range(2) for y in range(4) for c in range(2)
    ]
    return lax.ppermute(a, "col", perm)


def vmem():
    return pl.BlockSpec(memory_space=pltpu.VMEM)


def smem():
    return pl.BlockSpec(memory_space=pltpu.SMEM)


def block_ids(order, x, z):
    return jnp.stack([(x - dx + 4) % 4 * 4 + (z - dz + 4) % 4 for dx, dz in order]).astype(jnp.int32)


def order_inputs(place_z, place_x, own, other):
    def kernel(pz, px, own_ref, other_ref, z_ref, x_ref):
        for i in range(16):
            for places, out, low, size in ((pz, z_ref, 0, NZ), (px, x_ref, NZ, NX)):
                place = places[i]

                @pl.when(place < 8)
                def _():
                    out[pl.ds(i * size, size), :] = own_ref[place, pl.ds(low, size), :]

                @pl.when(place >= 8)
                def _():
                    out[pl.ds(i * size, size), :] = other_ref[place - 8, pl.ds(low, size), :]

    d = own.shape[-1]
    return pl.pallas_call(
        kernel,
        out_shape=(
            jax.ShapeDtypeStruct((16 * NZ, d), own.dtype),
            jax.ShapeDtypeStruct((16 * NX, d), own.dtype),
        ),
        in_specs=[smem(), smem(), vmem(), vmem()],
        out_specs=(vmem(), vmem()),
        compiler_params=pltpu.CompilerParams(vmem_limit_bytes=VMEM_LIMIT),
        cost_estimate=pl.CostEstimate(flops=0, bytes_accessed=4 * 1024 * 1024, transcendentals=0),
    )(place_z, place_x, own, other)


def input_grad_parts(slots, pieces, weight, rows):
    d, hidden = weight.shape
    n = len(pieces)

    def kernel(slot_ref, *refs):
        w_ref, send_ref, keep_ref = refs[n:]
        blocks = [(r, k) for r in refs[:n] for k in range(r.shape[0] // rows)]
        per = len(blocks) // 4
        for g in range(4):
            group = blocks[g * per:(g + 1) * per]
            panel = jnp.concatenate([r[k * rows:(k + 1) * rows, :] for r, k in group], axis=0)
            sums = lax.dot_general(
                panel, w_ref[...], (((1,), (1,)), ((), ())), preferred_element_type=jnp.float32
            )
            for k in range(per):
                part = sums[k * rows:(k + 1) * rows]
                slot = slot_ref[g * per + k]

                @pl.when(slot < 8)
                def _():
                    send_ref[slot] = part.astype(jnp.bfloat16)

                @pl.when(slot >= 8)
                def _():
                    keep_ref[slot - 8] = part

    return pl.pallas_call(
        kernel,
        out_shape=(
            jax.ShapeDtypeStruct((8, rows, d), jnp.bfloat16),
            jax.ShapeDtypeStruct((8, rows, d), jnp.float32),
        ),
        in_specs=[smem()] + [vmem()] * (n + 1),
        out_specs=(vmem(), vmem()),
        compiler_params=pltpu.CompilerParams(vmem_limit_bytes=VMEM_LIMIT),
        cost_estimate=pl.CostEstimate(
            flops=2 * 16 * rows * d * hidden, bytes_accessed=16 * rows * hidden * 2, transcendentals=0
        ),
    )(slots, *pieces, weight)


def weight_grad_of(inputs_z, inputs_x, pieces_z, pieces_x, tile=512):
    d = inputs_z.shape[1]
    hidden = pieces_z[0].shape[1]
    pieces = [*pieces_z, *pieces_x]
    n = len(pieces)

    def kernel(iz_ref, ix_ref, *refs):
        out_ref = refs[n]
        left = jnp.concatenate([iz_ref[...], ix_ref[...]], axis=0)
        right = jnp.concatenate([r[...] for r in refs[:n]], axis=0)
        out_ref[...] = lax.dot_general(
            left, right, (((0,), (0,)), ((), ())), preferred_element_type=jnp.float32
        ).astype(jnp.bfloat16)

    return pl.pallas_call(
        kernel,
        grid=(hidden // tile,),
        out_shape=jax.ShapeDtypeStruct((d, hidden), jnp.bfloat16),
        in_specs=[pl.BlockSpec(a.shape, lambda j: (0, 0)) for a in (inputs_z, inputs_x)]
        + [pl.BlockSpec((p.shape[0], tile), lambda j: (0, j)) for p in pieces],
        out_specs=pl.BlockSpec((d, tile), lambda j: (0, j)),
        compiler_params=pltpu.CompilerParams(vmem_limit_bytes=VMEM_LIMIT),
        cost_estimate=pl.CostEstimate(
            flops=2 * 2048 * d * hidden, bytes_accessed=12 * 1024 * 1024, transcendentals=0
        ),
    )(inputs_z, inputs_x, *pieces)


def reduce_rows(send, keep, l, y):
    got = along_col(send, 0, 0, 1)
    sums = (keep + got.astype(jnp.float32)).reshape(2, 4, *keep.shape[1:])

    def pick(a, axis, i):
        return lax.dynamic_index_in_dim(a, i, axis, keepdims=False)

    terms = [
        along_col(pick(sums, 1, (y + dy) % 4).astype(jnp.bfloat16), 0, dy, 0) for dy in (1, 3, 2)
    ]
    total = pick(sums, 1, y)
    for term in terms:
        total = total + term.astype(jnp.float32)
    last = along_col(pick(total, 0, 1 - l).astype(jnp.bfloat16), 1, 0, 0)
    return (pick(total, 0, l) + last.astype(jnp.float32)).astype(jnp.bfloat16)


def local(inputs, preact, out_grad, weight):
    row, col = lax.axis_index("row"), lax.axis_index("col")
    x, z = row // 4, row % 4
    l, y, c = col // 8, col // 2 % 4, col % 2

    pair = jnp.stack([inputs, along_col(inputs, 1, 0, 0)])
    own = jnp.concatenate(
        [pair, along_col(pair, 0, 1, 0), along_col(pair, 0, 2, 0), along_col(pair, 0, 3, 0)]
    )
    other = along_col(own, 0, 0, 1)

    grad = (out_grad.astype(jnp.float32) * gelu_slope(preact)).astype(jnp.bfloat16)
    gz, gx = grad[:NZ], grad[NZ:]
    half = NZ // 2
    a1, a3 = along_row(grad, 1, 0), along_row(grad, 3, 0)
    b1, b3 = along_row(gz, 0, 1), along_row(gz, 0, 3)
    a2 = jnp.concatenate(
        [along_row(a1[:ROWS // 2], 1, 0), along_row(a3[ROWS // 2:], 3, 0)], axis=0
    )
    b2 = jnp.concatenate([along_row(b1[:half], 0, 1), along_row(b3[half:], 0, 3)], axis=0)
    b13 = jnp.concatenate([b1, b3], axis=0)
    f1, f3 = along_row(b13, 1, 0), along_row(b13, 3, 0)
    xs = jnp.concatenate([gx, a1[NZ:], a3[NZ:], a2[NZ:]], axis=0)
    e1, e3 = along_row(xs, 0, 1), along_row(xs, 0, 3)
    p1 = along_row(jnp.concatenate([b2, f1[:NZ]], axis=0), 1, 0)
    p3 = along_row(jnp.concatenate([b2, f3[NZ:]], axis=0), 3, 0)
    p2 = along_row(b2, 2, 0)
    q1, q3 = along_row(e1[:2 * NX], 0, 1), along_row(e3[2 * NX:], 0, 3)

    pieces_z = [gz, a1[:NZ], a3[:NZ], a2[:NZ], b1, b3, b2, p2, f1, f3, p1, p3]
    pieces_x = [xs, e1, e3, q1, q3]

    ids_z, ids_x = block_ids(ORDER_Z, x, z), block_ids(ORDER_X, x, z)

    def place(ids):
        return (c - ids % 2 + 2) % 2 * 8 + (y - ids // 2 % 4 + 4) % 4 * 2 + (l - ids // 8 + 2) % 2

    def slot(ids):
        return jnp.where(ids % 2 == c, 8, 0) + ids // 2

    inputs_z, inputs_x = order_inputs(place(ids_z), place(ids_x), own, other)
    send_z, keep_z = input_grad_parts(slot(ids_z), pieces_z, weight, NZ)
    send_x, keep_x = input_grad_parts(slot(ids_x), pieces_x, weight, NX)
    weight_grad = weight_grad_of(inputs_z, inputs_x, pieces_z, pieces_x)
    input_grad = jnp.concatenate(
        [reduce_rows(send_z, keep_z, l, y), reduce_rows(send_x, keep_x, l, y)], axis=0
    )
    return (input_grad, weight_grad)


def solution(mesh):
    in_specs = (P("col", "row"), P("row", "col"), P("row", "col"), P("row", "col"))
    out_specs = (P("col", "row"), P("row", "col"))
    return jax.shard_map(local, mesh=mesh, in_specs=in_specs, out_specs=out_specs, check_vma=False)
```

```python
import math

import jax
import jax.numpy as jnp
from jax import lax
from jax.experimental import pallas as pl
from jax.experimental.pallas import tpu as pltpu
from jax.sharding import PartitionSpec as P

ROWS = 128
NZ = 96
NX = ROWS - NZ
VMEM_LIMIT = 16 * 1024 * 1024

ORDER_Z = ((0, 0), (1, 0), (3, 0), (2, 0), (0, 1), (0, 3), (0, 2),
           (1, 1), (1, 3), (3, 1), (3, 3), (2, 2), (1, 2), (2, 1), (3, 2), (2, 3))
ORDER_X = tuple((dx, dz) for dz in (0, 1, 3, 2) for dx in (0, 1, 3, 2))


def gelu_slope(preact):
    h = preact.astype(jnp.float32)
    scale_c = math.sqrt(2.0 / math.pi)
    t = jnp.tanh(scale_c * (h + 0.044715 * h * h * h))
    return 0.5 * (1.0 + t) + 0.5 * h * (1.0 - t * t) * scale_c * (1.0 + 3.0 * 0.044715 * h * h)


def along_row(a, dx, dz, name):
    perm = [(x * 4 + z, (x + dx) % 4 * 4 + (z + dz) % 4) for x in range(4) for z in range(4)]
    with jax.named_scope("ff_" + name):
        return lax.ppermute(a, "row", perm)


def along_col(a, dl, dy, dc, name):
    perm = [
        (l * 8 + y * 2 + c, (l + dl) % 2 * 8 + (y + dy) % 4 * 2 + (c + dc) % 2)
        for l in range(2) for y in range(4) for c in range(2)
    ]
    with jax.named_scope("ff_" + name):
        return lax.ppermute(a, "col", perm)


def swap_y(a, dy, name):
    perm = [(l * 8 + y * 2 + c, l * 8 + (y ^ dy) * 2 + c) for l in range(2) for y in range(4) for c in range(2)]
    with jax.named_scope("ff_" + name):
        return lax.ppermute(a, "col", perm)


def vmem():
    return pl.BlockSpec(memory_space=pltpu.VMEM)


def smem():
    return pl.BlockSpec(memory_space=pltpu.SMEM)


def block_ids(order, x, z):
    return jnp.stack([(x - dx + 4) % 4 * 4 + (z - dz + 4) % 4 for dx, dz in order]).astype(jnp.int32)


def hbm():
    return pl.BlockSpec(memory_space=pl.ANY)


def tied(a, *before):
    return lax.optimization_barrier((a, *before))


def order_inputs(place_z, place_x, own, other):
    def kernel(pz, px, own_ref, other_ref, out_ref, rows_ref):
        low_x = 16 * NZ
        for i in range(16):
            for places, low, size, at in ((pz, 0, NZ, i * NZ), (px, NZ, NX, low_x + i * NX)):
                place = places[i]

                @pl.when(place < 8)
                def _():
                    rows_ref[at:at + size, :] = own_ref[place, low:low + size, :]

                @pl.when(place >= 8)
                def _():
                    rows_ref[at:at + size, :] = other_ref[place - 8, low:low + size, :]

        out_ref[...] = rows_ref[...].T

    d = own.shape[-1]
    return pl.pallas_call(
        kernel,
        out_shape=jax.ShapeDtypeStruct((d, 16 * ROWS), own.dtype),
        in_specs=[smem(), smem(), vmem(), vmem()],
        out_specs=vmem(),
        scratch_shapes=[pltpu.VMEM((16 * ROWS, d), own.dtype)],
        compiler_params=pltpu.CompilerParams(vmem_limit_bytes=VMEM_LIMIT),
        cost_estimate=pl.CostEstimate(flops=0, bytes_accessed=0, transcendentals=0),
    )(place_z, place_x, own, other)


def input_grad_parts(slots, groups, weight, into=None):
    d, hidden = weight.shape
    n = len(groups)
    blocks = [(i, k, per, at) for i, (_, _, size, per, at) in enumerate(groups) for k in range(size // per)]

    def kernel(slot_ref, *refs):
        w_ref = refs[n]
        send_ref, keep_ref = refs[-2:]
        panel = jnp.concatenate(
            [r[low:low + size, :] for r, (_, low, size, _, _) in zip(refs, groups)], axis=0
        )
        sums = lax.dot_general(
            panel, w_ref[...], (((1,), (1,)), ((), ())), preferred_element_type=jnp.float32
        )
        row = 0
        for number, (_, _, per, at) in enumerate(blocks):
            part = sums[row:row + per]
            slot = slot_ref[number]

            @pl.when(slot < 8)
            def _():
                send_ref[slot, at:at + per, :] = part.astype(jnp.bfloat16)

            @pl.when(slot >= 8)
            def _():
                keep_ref[slot - 8, at:at + per, :] = part

            row += per

    extra = [] if into is None else list(into)
    return pl.pallas_call(
        kernel,
        out_shape=(
            jax.ShapeDtypeStruct((8, ROWS, d), jnp.bfloat16),
            jax.ShapeDtypeStruct((8, ROWS, d), jnp.float32),
        ),
        in_specs=[smem()] + [vmem()] * (n + 1 + len(extra)),
        out_specs=(vmem(), vmem()),
        input_output_aliases={n + 2: 0, n + 3: 1} if extra else {},
        compiler_params=pltpu.CompilerParams(vmem_limit_bytes=VMEM_LIMIT),
        cost_estimate=pl.CostEstimate(flops=0, bytes_accessed=0, transcendentals=0),
    )(slots, *[g[0] for g in groups], weight, *extra)


def weight_grad_of(inputs, pieces, tile=512):
    d, rows = inputs.shape
    hidden = pieces[0][0].shape[1]
    n, tiles = len(pieces), pieces[0][0].shape[1] // tile

    def kernel(in_ref, *refs):
        out_ref, right, result, sem, out_sem = refs[n:]

        def copies(j):
            at, found = 0, []
            for i, (_, low, size) in enumerate(pieces):
                found.append(pltpu.make_async_copy(
                    refs[i].at[pl.ds(low, size), pl.ds(j * tile, tile)],
                    right.at[j % 2, pl.ds(at, size), :],
                    sem.at[j % 2, i],
                ))
                at += size
            return found

        def leave(j):
            return pltpu.make_async_copy(
                result.at[j], out_ref.at[:, pl.ds(j * tile, tile)], out_sem.at[j]
            )

        for copy in copies(0):
            copy.start()
        for j in range(tiles):
            if j + 1 < tiles:
                for copy in copies(j + 1):
                    copy.start()
            for copy in copies(j):
                copy.wait()
            result[j] = lax.dot_general(
                in_ref[...], right[j % 2], (((1,), (0,)), ((), ())), preferred_element_type=jnp.float32
            ).astype(jnp.bfloat16)
            leave(j).start()
        for j in range(tiles):
            leave(j).wait()

    return pl.pallas_call(
        kernel,
        out_shape=jax.ShapeDtypeStruct((d, hidden), jnp.bfloat16),
        in_specs=[vmem()] + [hbm()] * n,
        out_specs=hbm(),
        scratch_shapes=[
            pltpu.VMEM((2, rows, tile), jnp.bfloat16),
            pltpu.VMEM((tiles, d, tile), jnp.bfloat16),
            pltpu.SemaphoreType.DMA((2, n)),
            pltpu.SemaphoreType.DMA((tiles,)),
        ],
        compiler_params=pltpu.CompilerParams(vmem_limit_bytes=VMEM_LIMIT),
        cost_estimate=pl.CostEstimate(
            flops=2 * 2048 * d * hidden, bytes_accessed=12 * 1024 * 1024, transcendentals=0
        ),
    )(inputs, *[p for p, _, _ in pieces])


def over_cores(place, keep, got):
    _, rows, d = keep.shape

    def kernel(place_ref, keep_ref, got_ref, *outs):
        y = place_ref[1]
        for i, dy in enumerate((1, 3, 2, 0)):
            for q in range(2):
                slot = q * 4 + (y + dy) % 4
                outs[i][q] = (keep_ref[slot] + got_ref[slot].astype(jnp.float32)).astype(outs[i].dtype)

    return pl.pallas_call(
        kernel,
        out_shape=[jax.ShapeDtypeStruct((2, rows, d), jnp.bfloat16)] * 3
        + [jax.ShapeDtypeStruct((2, rows, d), jnp.float32)],
        in_specs=[smem(), vmem(), vmem()],
        out_specs=[vmem()] * 4,
        compiler_params=pltpu.CompilerParams(vmem_limit_bytes=VMEM_LIMIT),
        cost_estimate=pl.CostEstimate(flops=0, bytes_accessed=0, transcendentals=0),
    )(place, keep, got)


def over_y(place, own, terms):
    _, rows, d = own.shape

    def kernel(place_ref, own_ref, *refs):
        def total(i):
            found = own_ref[i]
            for ref in refs[:3]:
                found = found + ref[i].astype(jnp.float32)
            return found

        l = place_ref[0]
        refs[3][...] = total(1 - l).astype(jnp.bfloat16)
        refs[4][...] = total(l)

    return pl.pallas_call(
        kernel,
        out_shape=[jax.ShapeDtypeStruct((rows, d), t) for t in (jnp.bfloat16, jnp.float32)],
        in_specs=[smem()] + [vmem()] * 4,
        out_specs=[vmem()] * 2,
        compiler_params=pltpu.CompilerParams(vmem_limit_bytes=VMEM_LIMIT),
        cost_estimate=pl.CostEstimate(flops=0, bytes_accessed=0, transcendentals=0),
    )(place, own, *terms)


def local(inputs, preact, out_grad, weight):
    row, col = lax.axis_index("row"), lax.axis_index("col")
    x, z = row // 4, row % 4
    l, y, c = col // 8, col // 2 % 4, col % 2

    def grad_of(p, g):
        return (g.astype(jnp.float32) * gelu_slope(p)).astype(jnp.bfloat16)

    grad = grad_of(preact, out_grad)
    half = NZ // 32 * 16
    ids_z, ids_x = block_ids(ORDER_Z, x, z), block_ids(ORDER_X, x, z)

    def place(ids):
        return (c ^ ids % 2) * 8 + (y ^ ids // 2 % 4) * 2 + (l ^ ids // 8)

    def whole(*arrays):
        return [(a, 0, a.shape[0]) for a in arrays]

    slots_z = jnp.where(ids_z % 2 == c, 8, 0) + ids_z // 2
    slots_x = jnp.where(ids_x % 2 == c, 8, 0) + ids_x // 2

    def terms(into, z_blocks, z_pieces, x_blocks=None, x_pieces=()):
        groups = [(*p, min(NZ, p[2]), 0) for p in z_pieces] + [(*p, NX, NZ) for p in x_pieces]
        slots = slots_z[z_blocks] if z_pieces else slots_x[x_blocks]
        if z_pieces and x_pieces:
            slots = jnp.concatenate([slots, slots_x[x_blocks]])
        return input_grad_parts(slots, groups, weight, into)


    gz = grad[:NZ]
    a1, a3 = along_row(grad, 1, 0, "G1"), along_row(grad, 3, 0, "G3")
    pair = jnp.stack([inputs, along_col(inputs, 1, 0, 0, "Il")])
    gz, pair = tied(gz, pair)
    b1, b3 = along_row(gz, 0, 1, "Z1"), along_row(gz, 0, 3, "Z3")
    i1 = swap_y(pair, 1, "I1")
    u = along_row(a1[:ROWS // 2], 1, 0, "Gr1")
    v = along_row(a3[ROWS // 2:], 3, 0, "Gr3")
    b1, b3, a1, a3 = tied(b1, b3, a1, a3)
    s = along_row(b1[:half], 0, 1, "Zr1")
    t = along_row(b3[half:], 0, 3, "Zr3")
    b13 = jnp.concatenate([b1, b3], axis=0)
    b13, u, v = tied(b13, u, v)
    f1, f3 = along_row(b13, 1, 0, "F1"), along_row(b13, 3, 0, "F3")
    near = jnp.concatenate([pair, i1])
    own = jnp.concatenate([near, swap_y(near, 2, "I2")])
    a2 = jnp.concatenate([u, v[:NZ - ROWS // 2]], axis=0)
    into = terms(None, slice(0, 4), [(gz, 0, NZ), (a1, 0, NZ), (a3, 0, NZ), *whole(a2)])
    xs = jnp.concatenate([grad[NZ:], a1[NZ:], a3[NZ:], v[NZ - ROWS // 2:]], axis=0)
    xs, s, t, own, *into = tied(xs, s, t, own, *into)
    e1, e3 = along_row(xs, 0, 1, "X1"), along_row(xs, 0, 3, "X3")
    b2 = jnp.concatenate([s, t], axis=0)
    p2 = along_row(b2, 2, 0, "P2")
    p1 = along_row(jnp.concatenate([b2, f1[:NZ]], axis=0), 1, 0, "P1")
    p3 = along_row(jnp.concatenate([b2, f3[NZ:]], axis=0), 3, 0, "P3")
    into = terms(into, slice(4, 11), whole(b1, b3, b2, f1, f3))
    e1, e3, f1, f3, *into = tied(e1, e3, f1, f3, *into)
    q1 = along_row(e1[:2 * NX], 0, 1, "Xr1")
    q3 = along_row(e3[2 * NX:], 0, 3, "Xr3")
    own, p1, p3 = tied(own, p1, p3)
    other = along_col(own, 0, 0, 1, "Ic")
    into = terms(into, None, [], slice(0, 12), whole(xs, e1, e3))
    turned = order_inputs(place(ids_z), place(ids_x), own, other)
    p1, p3, *into = tied(p1, p3, *into)
    send, keep = terms(into, slice(11, 16), whole(p2, p1, p3), slice(12, 16), whole(q1, q3))

    at = jnp.stack([l, y]).astype(jnp.int32)
    got = along_col(send, 0, 0, 1, "Rc")
    got, turned = tied(got, turned)
    *parts, rest = over_cores(at, keep, got)
    got = [along_col(t, 0, dy, 0, f"Ry{dy}") for t, dy in zip(parts, (1, 3, 2))]
    turned, rest = tied(turned, rest)
    pieces = [(gz, 0, NZ), (a1, 0, NZ), (a3, 0, NZ), *whole(a2, b1, b3, b2, f1, f3, p2, p1, p3, xs, e1, e3, q1, q3)]
    weight_grad = weight_grad_of(turned, pieces)
    *got, weight_grad = tied(*got, weight_grad)
    leaving, staying = over_y(at, rest, got)
    last = along_col(leaving, 1, 0, 0, "Rl")
    input_grad = (staying + last.astype(jnp.float32)).astype(jnp.bfloat16)
    return (input_grad, weight_grad)


def solution(mesh):
    in_specs = (P("col", "row"), P("row", "col"), P("row", "col"), P("row", "col"))
    out_specs = (P("col", "row"), P("row", "col"))
    return jax.shard_map(local, mesh=mesh, in_specs=in_specs, out_specs=out_specs, check_vma=False)
```

```python
import math

import jax
import jax.numpy as jnp
from jax import lax
from jax.experimental import pallas as pl
from jax.experimental.pallas import tpu as pltpu
from jax.sharding import PartitionSpec as P

ROWS = 128
NZ = 96
NX = ROWS - NZ
VMEM_LIMIT = 16 * 1024 * 1024

ORDER_Z = ((0, 0), (1, 0), (3, 0), (2, 0), (0, 1), (0, 3), (0, 2),
           (1, 1), (1, 3), (3, 1), (3, 3), (2, 2), (1, 2), (2, 1), (3, 2), (2, 3))
ORDER_X = tuple((dx, dz) for dz in (0, 1, 3, 2) for dx in (0, 1, 3, 2))


def gelu_slope(preact):
    h = preact.astype(jnp.float32)
    scale_c = math.sqrt(2.0 / math.pi)
    t = jnp.tanh(scale_c * (h + 0.044715 * h * h * h))
    return 0.5 * (1.0 + t) + 0.5 * h * (1.0 - t * t) * scale_c * (1.0 + 3.0 * 0.044715 * h * h)


def along_row(a, dx, dz, name):
    perm = [(x * 4 + z, (x + dx) % 4 * 4 + (z + dz) % 4) for x in range(4) for z in range(4)]
    with jax.named_scope("ff_" + name):
        return lax.ppermute(a, "row", perm)


def along_col(a, dl, dy, dc, name):
    perm = [
        (l * 8 + y * 2 + c, (l + dl) % 2 * 8 + (y + dy) % 4 * 2 + (c + dc) % 2)
        for l in range(2) for y in range(4) for c in range(2)
    ]
    with jax.named_scope("ff_" + name):
        return lax.ppermute(a, "col", perm)


def swap_y(a, dy, name):
    perm = [(l * 8 + y * 2 + c, l * 8 + (y ^ dy) * 2 + c) for l in range(2) for y in range(4) for c in range(2)]
    with jax.named_scope("ff_" + name):
        return lax.ppermute(a, "col", perm)


def vmem():
    return pl.BlockSpec(memory_space=pltpu.VMEM)


def smem():
    return pl.BlockSpec(memory_space=pltpu.SMEM)


def block_ids(order, x, z):
    return jnp.stack([(x - dx + 4) % 4 * 4 + (z - dz + 4) % 4 for dx, dz in order]).astype(jnp.int32)


def hbm():
    return pl.BlockSpec(memory_space=pl.ANY)


def tied(a, *before):
    return lax.optimization_barrier((a, *before))


def order_inputs(place_z, place_x, own, other):
    def kernel(pz, px, own_ref, other_ref, out_ref, rows_ref):
        low_x = 16 * NZ
        for i in range(16):
            for places, low, size, at in ((pz, 0, NZ, i * NZ), (px, NZ, NX, low_x + i * NX)):
                place = places[i]

                @pl.when(place < 8)
                def _():
                    rows_ref[at:at + size, :] = own_ref[place, low:low + size, :]

                @pl.when(place >= 8)
                def _():
                    rows_ref[at:at + size, :] = other_ref[place - 8, low:low + size, :]

        out_ref[...] = rows_ref[...].T

    d = own.shape[-1]
    return pl.pallas_call(
        kernel,
        out_shape=jax.ShapeDtypeStruct((d, 16 * ROWS), own.dtype),
        in_specs=[smem(), smem(), vmem(), vmem()],
        out_specs=vmem(),
        scratch_shapes=[pltpu.VMEM((16 * ROWS, d), own.dtype)],
        compiler_params=pltpu.CompilerParams(vmem_limit_bytes=VMEM_LIMIT),
        cost_estimate=pl.CostEstimate(flops=0, bytes_accessed=0, transcendentals=0),
    )(place_z, place_x, own, other)


def input_grad_parts(slots, groups, weight, into=None):
    d, hidden = weight.shape
    n = len(groups)
    blocks = [(i, k, per, at) for i, (_, _, size, per, at) in enumerate(groups) for k in range(size // per)]

    def kernel(slot_ref, *refs):
        w_ref = refs[n]
        send_ref, keep_ref = refs[-2:]
        panel = jnp.concatenate(
            [r[low:low + size, :] for r, (_, low, size, _, _) in zip(refs, groups)], axis=0
        )
        sums = lax.dot_general(
            panel, w_ref[...], (((1,), (1,)), ((), ())), preferred_element_type=jnp.float32
        )
        row = 0
        for number, (_, _, per, at) in enumerate(blocks):
            part = sums[row:row + per]
            slot = slot_ref[number]

            @pl.when(slot < 8)
            def _():
                send_ref[slot, at:at + per, :] = part.astype(jnp.bfloat16)

            @pl.when(slot >= 8)
            def _():
                keep_ref[slot - 8, at:at + per, :] = part

            row += per

    extra = [] if into is None else list(into)
    return pl.pallas_call(
        kernel,
        out_shape=(
            jax.ShapeDtypeStruct((8, ROWS, d), jnp.bfloat16),
            jax.ShapeDtypeStruct((8, ROWS, d), jnp.float32),
        ),
        in_specs=[smem()] + [vmem()] * (n + 1 + len(extra)),
        out_specs=(vmem(), vmem()),
        input_output_aliases={n + 2: 0, n + 3: 1} if extra else {},
        compiler_params=pltpu.CompilerParams(vmem_limit_bytes=VMEM_LIMIT),
        cost_estimate=pl.CostEstimate(flops=0, bytes_accessed=0, transcendentals=0),
    )(slots, *[g[0] for g in groups], weight, *extra)


def weight_grad_of(inputs, pieces, tile=512):
    d, rows = inputs.shape
    hidden = pieces[0][0].shape[1]
    n, tiles = len(pieces), pieces[0][0].shape[1] // tile

    def kernel(in_ref, *refs):
        out_ref, right, result, sem, out_sem = refs[n:]

        def copies(j):
            at, found = 0, []
            for i, (_, low, size) in enumerate(pieces):
                found.append(pltpu.make_async_copy(
                    refs[i].at[pl.ds(low, size), pl.ds(j * tile, tile)],
                    right.at[j % 2, pl.ds(at, size), :],
                    sem.at[j % 2, i],
                ))
                at += size
            return found

        def leave(j):
            return pltpu.make_async_copy(
                result.at[j], out_ref.at[:, pl.ds(j * tile, tile)], out_sem.at[j]
            )

        for copy in copies(0):
            copy.start()
        for j in range(tiles):
            if j + 1 < tiles:
                for copy in copies(j + 1):
                    copy.start()
            for copy in copies(j):
                copy.wait()
            result[j] = lax.dot_general(
                in_ref[...], right[j % 2], (((1,), (0,)), ((), ())), preferred_element_type=jnp.float32
            ).astype(jnp.bfloat16)
            leave(j).start()
        for j in range(tiles):
            leave(j).wait()

    return pl.pallas_call(
        kernel,
        out_shape=jax.ShapeDtypeStruct((d, hidden), jnp.bfloat16),
        in_specs=[vmem()] + [hbm()] * n,
        out_specs=hbm(),
        scratch_shapes=[
            pltpu.VMEM((2, rows, tile), jnp.bfloat16),
            pltpu.VMEM((tiles, d, tile), jnp.bfloat16),
            pltpu.SemaphoreType.DMA((2, n)),
            pltpu.SemaphoreType.DMA((tiles,)),
        ],
        compiler_params=pltpu.CompilerParams(vmem_limit_bytes=VMEM_LIMIT),
        cost_estimate=pl.CostEstimate(
            flops=2 * 2048 * d * hidden, bytes_accessed=12 * 1024 * 1024, transcendentals=0
        ),
    )(inputs, *[p for p, _, _ in pieces])


def over_cores(place, keep, got):
    _, rows, d = keep.shape

    def kernel(place_ref, keep_ref, got_ref, *outs):
        y = place_ref[1]
        for i, dy in enumerate((1, 3, 2, 0)):
            for q in range(2):
                slot = q * 4 + (y + dy) % 4
                outs[i][q] = (keep_ref[slot] + got_ref[slot].astype(jnp.float32)).astype(outs[i].dtype)

    return pl.pallas_call(
        kernel,
        out_shape=[jax.ShapeDtypeStruct((2, rows, d), jnp.bfloat16)] * 3
        + [jax.ShapeDtypeStruct((2, rows, d), jnp.float32)],
        in_specs=[smem(), vmem(), vmem()],
        out_specs=[vmem()] * 4,
        compiler_params=pltpu.CompilerParams(vmem_limit_bytes=VMEM_LIMIT),
        cost_estimate=pl.CostEstimate(flops=0, bytes_accessed=0, transcendentals=0),
    )(place, keep, got)


def over_y(place, own, terms):
    _, rows, d = own.shape

    def kernel(place_ref, own_ref, *refs):
        def total(i):
            found = own_ref[i]
            for ref in refs[:3]:
                found = found + ref[i].astype(jnp.float32)
            return found

        l = place_ref[0]
        refs[3][...] = total(1 - l).astype(jnp.bfloat16)
        refs[4][...] = total(l)

    return pl.pallas_call(
        kernel,
        out_shape=[jax.ShapeDtypeStruct((rows, d), t) for t in (jnp.bfloat16, jnp.float32)],
        in_specs=[smem()] + [vmem()] * 4,
        out_specs=[vmem()] * 2,
        compiler_params=pltpu.CompilerParams(vmem_limit_bytes=VMEM_LIMIT),
        cost_estimate=pl.CostEstimate(flops=0, bytes_accessed=0, transcendentals=0),
    )(place, own, *terms)


def local(inputs, preact, out_grad, weight):
    row, col = lax.axis_index("row"), lax.axis_index("col")
    x, z = row // 4, row % 4
    l, y, c = col // 8, col // 2 % 4, col % 2

    def grad_of(p, g):
        return (g.astype(jnp.float32) * gelu_slope(p)).astype(jnp.bfloat16)

    grad = grad_of(preact, out_grad)
    half = NZ // 32 * 16
    ids_z, ids_x = block_ids(ORDER_Z, x, z), block_ids(ORDER_X, x, z)

    def place(ids):
        return (c ^ ids % 2) * 8 + (y ^ ids // 2 % 4) * 2 + (l ^ ids // 8)

    def whole(*arrays):
        return [(a, 0, a.shape[0]) for a in arrays]

    slots_z = jnp.where(ids_z % 2 == c, 8, 0) + ids_z // 2
    slots_x = jnp.where(ids_x % 2 == c, 8, 0) + ids_x // 2

    def terms(into, z_blocks, z_pieces, x_blocks=None, x_pieces=()):
        groups = [(*p, min(NZ, p[2]), 0) for p in z_pieces] + [(*p, NX, NZ) for p in x_pieces]
        slots = slots_z[z_blocks] if z_pieces else slots_x[x_blocks]
        if z_pieces and x_pieces:
            slots = jnp.concatenate([slots, slots_x[x_blocks]])
        return input_grad_parts(slots, groups, weight, into)


    gz = grad[:NZ]
    a1, a3 = along_row(grad, 1, 0, "G1"), along_row(grad, 3, 0, "G3")
    pair = jnp.stack([inputs, along_col(inputs, 1, 0, 0, "Il")])
    b1, b3 = along_row(gz, 0, 1, "Z1"), along_row(gz, 0, 3, "Z3")
    u = along_row(a1[:ROWS // 2], 1, 0, "Gr1")
    v = along_row(a3[ROWS // 2:], 3, 0, "Gr3")
    pair, a1 = tied(pair, a1)
    i1 = swap_y(pair, 1, "I1")
    b1, b3, a1, a3 = tied(b1, b3, a1, a3)
    s = along_row(b1[:half], 0, 1, "Zr1")
    t = along_row(b3[half:], 0, 3, "Zr3")
    b13 = jnp.concatenate([b1, b3], axis=0)
    b13, u, v = tied(b13, u, v)
    f1, f3 = along_row(b13, 1, 0, "F1"), along_row(b13, 3, 0, "F3")
    near = jnp.concatenate([pair, i1])
    own = jnp.concatenate([near, swap_y(near, 2, "I2")])
    a2 = jnp.concatenate([u, v[:NZ - ROWS // 2]], axis=0)
    into = terms(None, slice(0, 4), [(gz, 0, NZ), (a1, 0, NZ), (a3, 0, NZ), *whole(a2)])
    xs = jnp.concatenate([grad[NZ:], a1[NZ:], a3[NZ:], v[NZ - ROWS // 2:]], axis=0)
    xs, s, t, *into = tied(xs, s, t, *into)
    e1, e3 = along_row(xs, 0, 1, "X1"), along_row(xs, 0, 3, "X3")
    b2 = jnp.concatenate([s, t], axis=0)
    p2 = along_row(b2, 2, 0, "P2")
    p1 = along_row(jnp.concatenate([b2, f1[:NZ]], axis=0), 1, 0, "P1")
    p3 = along_row(jnp.concatenate([b2, f3[NZ:]], axis=0), 3, 0, "P3")
    into = terms(into, slice(4, 11), whole(b1, b3, b2, f1, f3))
    e1, e3, f1, f3, *into = tied(e1, e3, f1, f3, *into)
    q1 = along_row(e1[:2 * NX], 0, 1, "Xr1")
    q3 = along_row(e3[2 * NX:], 0, 3, "Xr3")
    own, p1, p3 = tied(own, p1, p3)
    other = along_col(own, 0, 0, 1, "Ic")
    into = terms(into, None, [], slice(0, 12), whole(xs, e1, e3))
    turned = order_inputs(place(ids_z), place(ids_x), own, other)
    p1, p3, *into = tied(p1, p3, *into)
    send, keep = terms(into, slice(11, 16), whole(p2, p1, p3), slice(12, 16), whole(q1, q3))

    at = jnp.stack([l, y]).astype(jnp.int32)
    got = along_col(send, 0, 0, 1, "Rc")
    got, turned = tied(got, turned)
    *parts, rest = over_cores(at, keep, got)
    got = [along_col(t, 0, dy, 0, f"Ry{dy}") for t, dy in zip(parts, (1, 3, 2))]
    turned, rest = tied(turned, rest)
    pieces = [(gz, 0, NZ), (a1, 0, NZ), (a3, 0, NZ), *whole(a2, b1, b3, b2, f1, f3, p2, p1, p3, xs, e1, e3, q1, q3)]
    weight_grad = weight_grad_of(turned, pieces)
    *got, weight_grad = tied(*got, weight_grad)
    leaving, staying = over_y(at, rest, got)
    last = along_col(leaving, 1, 0, 0, "Rl")
    input_grad = (staying + last.astype(jnp.float32)).astype(jnp.bfloat16)
    return (input_grad, weight_grad)


def solution(mesh):
    in_specs = (P("col", "row"), P("row", "col"), P("row", "col"), P("row", "col"))
    out_specs = (P("col", "row"), P("row", "col"))
    return jax.shard_map(local, mesh=mesh, in_specs=in_specs, out_specs=out_specs, check_vma=False)
```

```python
import math

import jax
import jax.numpy as jnp
from jax import lax
from jax.experimental import pallas as pl
from jax.experimental.pallas import tpu as pltpu
from jax.sharding import PartitionSpec as P

ROWS = 128
NZ = 96
NX = ROWS - NZ
VMEM_LIMIT = 16 * 1024 * 1024

ORDER_Z = ((0, 0), (1, 0), (3, 0), (2, 0), (0, 1), (0, 3), (0, 2),
           (1, 1), (1, 3), (3, 1), (3, 3), (2, 2), (1, 2), (2, 1), (3, 2), (2, 3))
ORDER_X = tuple((dx, dz) for dz in (0, 1, 3, 2) for dx in (0, 1, 3, 2))


def gelu_slope(preact):
    h = preact.astype(jnp.float32)
    scale_c = math.sqrt(2.0 / math.pi)
    t = jnp.tanh(scale_c * (h + 0.044715 * h * h * h))
    return 0.5 * (1.0 + t) + 0.5 * h * (1.0 - t * t) * scale_c * (1.0 + 3.0 * 0.044715 * h * h)


def along_row(a, dx, dz, name):
    perm = [(x * 4 + z, (x + dx) % 4 * 4 + (z + dz) % 4) for x in range(4) for z in range(4)]
    with jax.named_scope("ff_" + name):
        return lax.ppermute(a, "row", perm)


def along_col(a, dl, dy, dc, name):
    perm = [
        (l * 8 + y * 2 + c, (l + dl) % 2 * 8 + (y + dy) % 4 * 2 + (c + dc) % 2)
        for l in range(2) for y in range(4) for c in range(2)
    ]
    with jax.named_scope("ff_" + name):
        return lax.ppermute(a, "col", perm)


def swap_y(a, dy, name):
    perm = [(l * 8 + y * 2 + c, l * 8 + (y ^ dy) * 2 + c) for l in range(2) for y in range(4) for c in range(2)]
    with jax.named_scope("ff_" + name):
        return lax.ppermute(a, "col", perm)


def vmem():
    return pl.BlockSpec(memory_space=pltpu.VMEM)


def smem():
    return pl.BlockSpec(memory_space=pltpu.SMEM)


def block_ids(order, x, z):
    return jnp.stack([(x - dx + 4) % 4 * 4 + (z - dz + 4) % 4 for dx, dz in order]).astype(jnp.int32)


def hbm():
    return pl.BlockSpec(memory_space=pl.ANY)


def tied(a, *before):
    return lax.optimization_barrier((a, *before))


def order_inputs(place_z, place_x, own, other):
    def kernel(pz, px, own_ref, other_ref, out_ref, rows_ref):
        low_x = 16 * NZ
        for i in range(16):
            for places, low, size, at in ((pz, 0, NZ, i * NZ), (px, NZ, NX, low_x + i * NX)):
                place = places[i]

                @pl.when(place < 8)
                def _():
                    rows_ref[at:at + size, :] = own_ref[place, low:low + size, :]

                @pl.when(place >= 8)
                def _():
                    rows_ref[at:at + size, :] = other_ref[place - 8, low:low + size, :]

        out_ref[...] = rows_ref[...].T

    d = own.shape[-1]
    return pl.pallas_call(
        kernel,
        out_shape=jax.ShapeDtypeStruct((d, 16 * ROWS), own.dtype),
        in_specs=[smem(), smem(), vmem(), vmem()],
        out_specs=vmem(),
        scratch_shapes=[pltpu.VMEM((16 * ROWS, d), own.dtype)],
        compiler_params=pltpu.CompilerParams(vmem_limit_bytes=VMEM_LIMIT),
        cost_estimate=pl.CostEstimate(flops=0, bytes_accessed=0, transcendentals=0),
    )(place_z, place_x, own, other)


def input_grad_parts(slots, groups, weight, into=None):
    d, hidden = weight.shape
    n = len(groups)
    blocks = [(i, k, per, at) for i, (_, _, size, per, at) in enumerate(groups) for k in range(size // per)]

    def kernel(slot_ref, *refs):
        w_ref = refs[n]
        send_ref, keep_ref = refs[-2:]
        panel = jnp.concatenate(
            [r[low:low + size, :] for r, (_, low, size, _, _) in zip(refs, groups)], axis=0
        )
        sums = lax.dot_general(
            panel, w_ref[...], (((1,), (1,)), ((), ())), preferred_element_type=jnp.float32
        )
        row = 0
        for number, (_, _, per, at) in enumerate(blocks):
            part = sums[row:row + per]
            slot = slot_ref[number]

            @pl.when(slot < 8)
            def _():
                send_ref[slot, at:at + per, :] = part.astype(jnp.bfloat16)

            @pl.when(slot >= 8)
            def _():
                keep_ref[slot - 8, at:at + per, :] = part

            row += per

    extra = [] if into is None else list(into)
    return pl.pallas_call(
        kernel,
        out_shape=(
            jax.ShapeDtypeStruct((8, ROWS, d), jnp.bfloat16),
            jax.ShapeDtypeStruct((8, ROWS, d), jnp.float32),
        ),
        in_specs=[smem()] + [vmem()] * (n + 1 + len(extra)),
        out_specs=(vmem(), vmem()),
        input_output_aliases={n + 2: 0, n + 3: 1} if extra else {},
        compiler_params=pltpu.CompilerParams(vmem_limit_bytes=VMEM_LIMIT),
        cost_estimate=pl.CostEstimate(flops=0, bytes_accessed=0, transcendentals=0),
    )(slots, *[g[0] for g in groups], weight, *extra)


def weight_grad_of(inputs, pieces, tile=512):
    d, rows = inputs.shape
    hidden = pieces[0][0].shape[1]
    n, tiles = len(pieces), pieces[0][0].shape[1] // tile

    def kernel(in_ref, *refs):
        out_ref, right, result, sem, out_sem = refs[n:]

        def copies(j):
            at, found = 0, []
            for i, (_, low, size) in enumerate(pieces):
                found.append(pltpu.make_async_copy(
                    refs[i].at[pl.ds(low, size), pl.ds(j * tile, tile)],
                    right.at[j % 2, pl.ds(at, size), :],
                    sem.at[j % 2, i],
                ))
                at += size
            return found

        def leave(j):
            return pltpu.make_async_copy(
                result.at[j], out_ref.at[:, pl.ds(j * tile, tile)], out_sem.at[j]
            )

        for copy in copies(0):
            copy.start()
        for j in range(tiles):
            if j + 1 < tiles:
                for copy in copies(j + 1):
                    copy.start()
            for copy in copies(j):
                copy.wait()
            result[j] = lax.dot_general(
                in_ref[...], right[j % 2], (((1,), (0,)), ((), ())), preferred_element_type=jnp.float32
            ).astype(jnp.bfloat16)
            leave(j).start()
        for j in range(tiles):
            leave(j).wait()

    return pl.pallas_call(
        kernel,
        out_shape=jax.ShapeDtypeStruct((d, hidden), jnp.bfloat16),
        in_specs=[vmem()] + [hbm()] * n,
        out_specs=hbm(),
        scratch_shapes=[
            pltpu.VMEM((2, rows, tile), jnp.bfloat16),
            pltpu.VMEM((tiles, d, tile), jnp.bfloat16),
            pltpu.SemaphoreType.DMA((2, n)),
            pltpu.SemaphoreType.DMA((tiles,)),
        ],
        compiler_params=pltpu.CompilerParams(vmem_limit_bytes=VMEM_LIMIT),
        cost_estimate=pl.CostEstimate(
            flops=2 * 2048 * d * hidden, bytes_accessed=12 * 1024 * 1024, transcendentals=0
        ),
    )(inputs, *[p for p, _, _ in pieces])


def over_cores(place, keep, got):
    _, rows, d = keep.shape

    def kernel(place_ref, keep_ref, got_ref, *outs):
        y = place_ref[1]
        for i, dy in enumerate((1, 3, 2, 0)):
            for q in range(2):
                slot = q * 4 + (y + dy) % 4
                outs[i][q] = (keep_ref[slot] + got_ref[slot].astype(jnp.float32)).astype(outs[i].dtype)

    return pl.pallas_call(
        kernel,
        out_shape=[jax.ShapeDtypeStruct((2, rows, d), jnp.bfloat16)] * 3
        + [jax.ShapeDtypeStruct((2, rows, d), jnp.float32)],
        in_specs=[smem(), vmem(), vmem()],
        out_specs=[vmem()] * 4,
        compiler_params=pltpu.CompilerParams(vmem_limit_bytes=VMEM_LIMIT),
        cost_estimate=pl.CostEstimate(flops=0, bytes_accessed=0, transcendentals=0),
    )(place, keep, got)


def over_y(place, own, terms):
    _, rows, d = own.shape

    def kernel(place_ref, own_ref, *refs):
        def total(i):
            found = own_ref[i]
            for ref in refs[:3]:
                found = found + ref[i].astype(jnp.float32)
            return found

        l = place_ref[0]
        refs[3][...] = total(1 - l).astype(jnp.bfloat16)
        refs[4][...] = total(l)

    return pl.pallas_call(
        kernel,
        out_shape=[jax.ShapeDtypeStruct((rows, d), t) for t in (jnp.bfloat16, jnp.float32)],
        in_specs=[smem()] + [vmem()] * 4,
        out_specs=[vmem()] * 2,
        compiler_params=pltpu.CompilerParams(vmem_limit_bytes=VMEM_LIMIT),
        cost_estimate=pl.CostEstimate(flops=0, bytes_accessed=0, transcendentals=0),
    )(place, own, *terms)


def local(inputs, preact, out_grad, weight):
    row, col = lax.axis_index("row"), lax.axis_index("col")
    x, z = row // 4, row % 4
    l, y, c = col // 8, col // 2 % 4, col % 2

    def grad_of(p, g):
        return (g.astype(jnp.float32) * gelu_slope(p)).astype(jnp.bfloat16)

    grad = grad_of(preact, out_grad)
    half = NZ // 32 * 16
    ids_z, ids_x = block_ids(ORDER_Z, x, z), block_ids(ORDER_X, x, z)

    def place(ids):
        return (c ^ ids % 2) * 8 + (y ^ ids // 2 % 4) * 2 + (l ^ ids // 8)

    def whole(*arrays):
        return [(a, 0, a.shape[0]) for a in arrays]

    slots_z = jnp.where(ids_z % 2 == c, 8, 0) + ids_z // 2
    slots_x = jnp.where(ids_x % 2 == c, 8, 0) + ids_x // 2

    def terms(into, z_blocks, z_pieces, x_blocks=None, x_pieces=()):
        groups = [(*p, min(NZ, p[2]), 0) for p in z_pieces] + [(*p, NX, NZ) for p in x_pieces]
        slots = slots_z[z_blocks] if z_pieces else slots_x[x_blocks]
        if z_pieces and x_pieces:
            slots = jnp.concatenate([slots, slots_x[x_blocks]])
        return input_grad_parts(slots, groups, weight, into)


    gz = grad[:NZ]
    a1, a3 = along_row(grad, 1, 0, "G1"), along_row(grad, 3, 0, "G3")
    pair = jnp.stack([inputs, along_col(inputs, 1, 0, 0, "Il")])
    b1, b3 = along_row(gz, 0, 1, "Z1"), along_row(gz, 0, 3, "Z3")
    u = along_row(a1[:ROWS // 2], 1, 0, "Gr1")
    v = along_row(a3[ROWS // 2:], 3, 0, "Gr3")
    pair, a1 = tied(pair, a1)
    i1 = swap_y(pair, 1, "I1")
    b1, b3, a1, a3 = tied(b1, b3, a1, a3)
    s = along_row(b1[:half], 0, 1, "Zr1")
    t = along_row(b3[half:], 0, 3, "Zr3")
    b13 = jnp.concatenate([b1, b3], axis=0)
    b13, u, v = tied(b13, u, v)
    f1, f3 = along_row(b13, 1, 0, "F1"), along_row(b13, 3, 0, "F3")
    near = jnp.concatenate([pair, i1])
    own = jnp.concatenate([near, swap_y(near, 2, "I2")])
    a2 = jnp.concatenate([u, v[:NZ - ROWS // 2]], axis=0)
    into = terms(None, slice(0, 4), [(gz, 0, NZ), (a1, 0, NZ), (a3, 0, NZ), *whole(a2)])
    xs = jnp.concatenate([grad[NZ:], a1[NZ:], a3[NZ:], v[NZ - ROWS // 2:]], axis=0)
    xs, s, t, *into = tied(xs, s, t, *into)
    e1, e3 = along_row(xs, 0, 1, "X1"), along_row(xs, 0, 3, "X3")
    b2 = jnp.concatenate([s, t], axis=0)
    p2 = along_row(b2, 2, 0, "P2")
    p1 = along_row(jnp.concatenate([b2, f1[:NZ]], axis=0), 1, 0, "P1")
    p3 = along_row(jnp.concatenate([b2, f3[NZ:]], axis=0), 3, 0, "P3")
    into = terms(into, slice(4, 11), whole(b1, b3, b2, f1, f3))
    e1, e3, f1, f3 = tied(e1, e3, f1, f3)
    q1 = along_row(e1[:2 * NX], 0, 1, "Xr1")
    q3 = along_row(e3[2 * NX:], 0, 3, "Xr3")
    own, p1, p3 = tied(own, p1, p3)
    other = along_col(own, 0, 0, 1, "Ic")
    into = terms(into, None, [], slice(0, 12), whole(xs, e1, e3))
    turned = order_inputs(place(ids_z), place(ids_x), own, other)
    p1, p3, *into = tied(p1, p3, *into)
    send, keep = terms(into, slice(11, 16), whole(p2, p1, p3), slice(12, 16), whole(q1, q3))

    at = jnp.stack([l, y]).astype(jnp.int32)
    got = along_col(send, 0, 0, 1, "Rc")
    got, turned = tied(got, turned)
    *parts, rest = over_cores(at, keep, got)
    got = [along_col(t, 0, dy, 0, f"Ry{dy}") for t, dy in zip(parts, (1, 3, 2))]
    turned, rest = tied(turned, rest)
    pieces = [(gz, 0, NZ), (a1, 0, NZ), (a3, 0, NZ), *whole(a2, b1, b3, b2, f1, f3, p2, p1, p3, xs, e1, e3, q1, q3)]
    weight_grad = weight_grad_of(turned, pieces)
    *got, weight_grad = tied(*got, weight_grad)
    leaving, staying = over_y(at, rest, got)
    last = along_col(leaving, 1, 0, 0, "Rl")
    input_grad = (staying + last.astype(jnp.float32)).astype(jnp.bfloat16)
    return (input_grad, weight_grad)


def solution(mesh):
    in_specs = (P("col", "row"), P("row", "col"), P("row", "col"), P("row", "col"))
    out_specs = (P("col", "row"), P("row", "col"))
    return jax.shard_map(local, mesh=mesh, in_specs=in_specs, out_specs=out_specs, check_vma=False)
```
